32 devices in a mesh: head: 2 (over y), seq: 16 (over z, x, core).
Axes of the slice: x: 2, y: 2, z: 4, core: 2. Of those that a mesh axis runs over, the one named last changes fastest.
Arguments:
- queries: bfloat16 [16384, 2048], P('seq', 'head'), may hold values from -24 to 24
- key_rows: bfloat16 [16384, 2048], P('seq', 'head'), may hold values from -24 to 24
- value_rows: bfloat16 [16384, 2048], P('seq', 'head'), may hold values from -6 to 6
- token_rates: float32 [4, 16384], P('head', 'seq'), may hold values from 0.01 to 1
- gate_fast: float32 [4, 512, 512], P('head'), may hold values from -0.25 to 0.25
- lift_fast: float32 [4, 512, 512], P('head'), may hold values from -0.25 to 0.25
- down_fast: float32 [4, 512, 512], P('head'), may hold values from -0.25 to 0.25
- memory_gain: float32 [4, 512], P('head'), may hold values from 0.1 to 1
- out_weight: bfloat16 [2048, 2048], P('head'), may hold values from -0.125 to 0.125
Outputs:
- layer_out: bfloat16 [16384, 2048], P('seq', 'head')
The draws below stay inside these ranges and needn't reach their ends.
All inputs are finite; a program needn't handle non-finite values.
Results may differ from the reference program's by a relative error of at most 0.014.
Values may be sent and summed in bfloat16 or wider, within the bound.
A program may use at most 128 MiB of HBM per device.

```python
import math
import jax
import jax.numpy as jnp
from jax import lax

HEADS = 4
HEAD = 512
FH = 512
D = 2048
WINDOW = 1024
NS_STEPS = 2
TOK_DEV = 1024
TOKENS = 16384


def shared_rows(key):
    base_key = jax.random.fold_in(key, 4099)
    split_keys = jax.random.split(base_key, 5)
    query_draw = jax.random.truncated_normal(split_keys[0], -4.0, 4.0, (TOKENS, HEADS, HEAD), jnp.float32)
    key_draw = jax.random.truncated_normal(split_keys[1], -4.0, 4.0, (TOKENS, HEADS, HEAD), jnp.float32)
    common_part = jax.random.uniform(split_keys[4], (1, HEADS, HEAD), jnp.float32, -0.8, 0.8)
    key_draw = key_draw + common_part
    return (query_draw.reshape(TOKENS, D), key_draw.reshape(TOKENS, D))


def draw_queries(key, part):
    return shared_rows(key)[0].astype(jnp.bfloat16)


def draw_key_rows(key, part):
    return shared_rows(key)[1].astype(jnp.bfloat16)


def block_scale(own_key, extent, shards, low, high):
    factor_of, own = 1.0, jax.random.fold_in(own_key, 6)
    for axis_at, blocks in shards:
        steps = jnp.exp(jax.random.uniform(jax.random.fold_in(own, axis_at), (blocks,), jnp.float32, low / len(shards), high / len(shards)))
        factor_of = factor_of * jnp.repeat(steps, extent[axis_at] // blocks).reshape([-1 if axis == axis_at else 1 for axis in range(len(extent))])
    return factor_of


def noise(rng, shape, spread, limit, pieces=(), held_as=jnp.bfloat16):
    values = jax.random.normal(rng, shape, jnp.float32) * spread
    if len(pieces) > 0:
        values = block_scale(rng, shape, pieces, -0.22, 0.18) * values
    return jnp.clip(values, min=-limit, max=limit).astype(held_as)


def setup_inputs(seed: int = 0) -> dict:
    key_list = jax.random.split(jax.random.key(seed), 10)
    return {
        "queries": draw_queries(jax.random.fold_in(key_list[9], 71), 0),
        "key_rows": draw_key_rows(jax.random.fold_in(key_list[9], 71), 0),
        "value_rows": noise(key_list[2], (TOKENS, D), 1.0, 6.0, ((0, 16), (1, 2))),
        "token_rates": jnp.clip(jnp.exp(math.log(1.0) - 4.6051702 * jax.random.uniform(key_list[3], (HEADS, TOKENS), jnp.float32) ** block_scale(key_list[3], (HEADS, TOKENS), ((0, 2), (1, 16)), -0.2, 0.2)), 0.01, 1.0),
        "gate_fast": noise(key_list[4], (HEADS, HEAD, FH), HEAD ** -0.5, 0.25, ((0, 2),), jnp.float32),
        "lift_fast": noise(key_list[5], (HEADS, HEAD, FH), HEAD ** -0.5, 0.25, ((0, 2),), jnp.float32),
        "down_fast": noise(key_list[6], (HEADS, FH, HEAD), FH ** -0.5, 0.25, ((0, 2),), jnp.float32),
        "memory_gain": jnp.clip(jnp.exp(math.log(1.0) - 2.3025851 * jax.random.uniform(key_list[7], (HEADS, HEAD), jnp.float32) ** block_scale(key_list[7], (HEADS, HEAD), ((0, 2),), -0.2, 0.2)), 0.1, 1.0),
        "out_weight": noise(key_list[8], (D, D), D ** -0.5, 0.125, ((0, 2),)),
    }


COEF_A = 3.4445
COEF_B = -4.775
COEF_C = 2.0315
EPSILON = 1e-06

def rounded(values_in):
    return lax.optimization_barrier(values_in.astype(jnp.bfloat16))

def window_attention(queries, key_rows, value_rows):
    total_rows = queries.shape[0]
    block_rows = min(512, TOK_DEV)
    span_rows = block_rows + WINDOW
    padding = jnp.zeros((WINDOW, D), jnp.bfloat16)
    all_keys = jnp.concatenate([padding, key_rows], axis=0)
    all_values = jnp.concatenate([padding, value_rows], axis=0)
    score_scale = HEAD ** (-0.5)
    query_index = jnp.arange(block_rows, dtype=jnp.int32)[:, None]
    key_index = jnp.arange(span_rows, dtype=jnp.int32)[None, :]

    def one_block(start):
        query_block = lax.dynamic_slice_in_dim(queries, start, block_rows, 0).reshape(block_rows, HEADS, HEAD).astype(jnp.float32)
        key_block = lax.dynamic_slice_in_dim(all_keys, start, span_rows, 0).reshape(span_rows, HEADS, HEAD).astype(jnp.float32)
        value_block = lax.dynamic_slice_in_dim(all_values, start, span_rows, 0).reshape(span_rows, HEADS, HEAD).astype(jnp.float32)
        scores = jnp.einsum('qhd,khd->hqk', query_block, key_block) * score_scale
        allowed = (key_index > query_index) & (key_index <= query_index + WINDOW) & (start + key_index - WINDOW >= 0)
        scores = jnp.where(allowed[None, :, :], scores, -jnp.inf)
        largest = lax.optimization_barrier(jnp.max(scores, axis=2, keepdims=True))
        exponent = jnp.exp(scores - largest)
        probability = rounded(exponent / lax.optimization_barrier(jnp.sum(exponent, axis=2, keepdims=True))).astype(jnp.float32)
        attended = jnp.einsum('hqk,khd->qhd', probability, value_block)
        return attended.reshape(block_rows, D)
    starts = jnp.arange(total_rows // block_rows, dtype=jnp.int32) * block_rows
    return lax.map(one_block, starts).reshape(total_rows, D)

def orthogonal(gradient):
    column_gram = jnp.dot(gradient.T, gradient, precision=lax.Precision.HIGHEST)
    trace_sum = jnp.trace(column_gram) + EPSILON
    iterate = (gradient / jnp.sqrt(trace_sum)).astype(jnp.bfloat16)
    column_gram = column_gram / trace_sum
    identity = jnp.eye(column_gram.shape[0], dtype=jnp.float32)
    for sweep_index in range(NS_STEPS):
        gram_half = column_gram.astype(jnp.bfloat16)
        square = jnp.dot(gram_half, gram_half, preferred_element_type=jnp.float32)
        polynomial = (COEF_A * identity + COEF_B * column_gram + COEF_C * square).astype(jnp.bfloat16)
        iterate = jnp.dot(iterate, polynomial, preferred_element_type=jnp.float32).astype(jnp.bfloat16)
        if sweep_index + 1 < NS_STEPS:
            column_gram = jnp.dot(iterate.T, iterate, preferred_element_type=jnp.float32)
    return iterate

def renew(old_weight, update):
    change = old_weight - update.astype(jnp.float32)
    old_square = lax.optimization_barrier(jnp.sum(old_weight * old_weight, axis=0, keepdims=True))
    new_square = lax.optimization_barrier(jnp.sum(change * change, axis=0, keepdims=True))
    return (change * jnp.sqrt(old_square / (new_square + EPSILON))).astype(jnp.bfloat16)

def head_memory(key_head, value_head, query_head, rate_head, gate_fast, lift_fast, down_fast, memory_gain):
    gate_pre = jnp.dot(key_head, rounded(gate_fast), preferred_element_type=jnp.float32)
    lift_pre = jnp.dot(key_head, rounded(lift_fast), preferred_element_type=jnp.float32)
    sigmoid_gate = jax.nn.sigmoid(gate_pre)
    activated = gate_pre * sigmoid_gate
    hidden = (activated * lift_pre).astype(jnp.bfloat16)
    target = (-rate_head[:, None] * value_head.astype(jnp.float32)).astype(jnp.bfloat16)
    grad_down = jnp.dot(hidden.T, target, preferred_element_type=jnp.float32)
    back_hidden = jnp.dot(target, rounded(down_fast).T, preferred_element_type=jnp.float32)
    back_gate = (back_hidden * lift_pre * sigmoid_gate * (1.0 + gate_pre * (1.0 - sigmoid_gate))).astype(jnp.bfloat16)
    back_lift = (back_hidden * activated).astype(jnp.bfloat16)
    grad_gate = jnp.dot(key_head.T, back_gate, preferred_element_type=jnp.float32)
    grad_lift = jnp.dot(key_head.T, back_lift, preferred_element_type=jnp.float32)
    gate_new = renew(gate_fast, orthogonal(grad_gate))
    lift_new = renew(lift_fast, orthogonal(grad_lift))
    down_new = renew(down_fast, orthogonal(grad_down))
    gate_apply = jnp.dot(query_head, gate_new, preferred_element_type=jnp.float32)
    lift_apply = jnp.dot(query_head, lift_new, preferred_element_type=jnp.float32)
    hidden_apply = (jax.nn.silu(gate_apply) * lift_apply).astype(jnp.bfloat16)
    memory_out = jnp.dot(hidden_apply, down_new, preferred_element_type=jnp.float32)
    mean_square = lax.optimization_barrier(jnp.mean(memory_out * memory_out, axis=1, keepdims=True))
    return memory_out * lax.rsqrt(mean_square + EPSILON) * memory_gain[None, :]

def reference(queries, key_rows, value_rows, token_rates, gate_fast, lift_fast, down_fast, memory_gain, out_weight):
    attended = window_attention(queries, key_rows, value_rows)
    query_heads = queries.reshape(TOKENS, HEADS, HEAD).transpose(1, 0, 2)
    key_heads = key_rows.reshape(TOKENS, HEADS, HEAD).transpose(1, 0, 2)
    value_heads = value_rows.reshape(TOKENS, HEADS, HEAD).transpose(1, 0, 2)

    def one_head(items):
        return head_memory(items[0], items[1], items[2], items[3], items[4], items[5], items[6], items[7])
    memory = lax.map(one_head, (key_heads, value_heads, query_heads, token_rates, gate_fast, lift_fast, down_fast, memory_gain))
    memory_flat = memory.transpose(1, 0, 2).reshape(TOKENS, D)
    combined = (attended + memory_flat).astype(jnp.bfloat16)
    return jnp.dot(combined, out_weight, preferred_element_type=jnp.float32).astype(jnp.bfloat16)
```

```python
import functools

import jax
import jax.numpy as jnp
from jax import lax
from jax.experimental import pallas as pl
from jax.experimental.pallas import tpu as pltpu
from jax.sharding import PartitionSpec as P

HEAD = 512
WINDOW = 1024
NS_STEPS = 2
COEF_A = 3.4445
COEF_B = -4.775
COEF_C = 2.0315
EPSILON = 1e-06
MESH = pl.DeviceIdType.MESH
F32 = jnp.float32
BF16 = jnp.bfloat16
MASKED = -1e30


def dot(a, b, ca=1, cb=0):
    return lax.dot_general(a, b, (((ca,), (cb,)), ((), ())), preferred_element_type=F32)


def kernel(
    n, tokens, heads, out_cols,
    q_ref, k_ref, v_ref, rate_ref, gate_ref, lift_ref, down_ref, gain_ref, ow_ref, o_ref,
    ek, ev, grad, core_send, core_recv, rs_send, rs_recv, gsum, att, m_ref, l_ref, new_w,
    psend, precv,
    halo_s, halo_r, core_s, core_r, rs_s, rs_r, ag_s, ag_r, nw_s, nw_r, y_s, y_r,
):
    me = lax.axis_index("seq")
    y = lax.axis_index("head")
    rows3 = 3 * HEAD
    core = me % 2
    steps = []
    d = 2
    while d < n:
        steps.append(d)
        d *= 2
    steps = steps[1:] + steps[:1]

    def bit(d):
        return (me // d) % 2

    def partner(d):
        return me + d * (1 - 2 * bit(d))

    barrier = pltpu.get_barrier_semaphore()
    peers = [{"seq": (me + 1) % n}, {"seq": (me + n - 1) % n}, {"head": 1 - y}]
    peers += [{"seq": partner(d)} for d in [1] + steps]
    for peer in peers:
        pl.semaphore_signal(barrier, inc=1, device_id=peer, device_id_type=MESH)
    pl.semaphore_wait(barrier, len(peers))

    def halo_copies(h):
        cols = pl.ds(h * HEAD, HEAD)
        return [
            pltpu.make_async_remote_copy(
                src_ref=src.at[:, cols], dst_ref=dst.at[:, cols],
                send_sem=halo_s.at[2 * h + j], recv_sem=halo_r.at[2 * h + j],
                device_id={"seq": (me + 1) % n}, device_id_type=MESH,
            )
            for j, (src, dst) in enumerate(((k_ref, ek), (v_ref, ev)))
        ]

    @pl.when(me < n - 1)
    def _():
        for h in range(heads):
            for c in halo_copies(h):
                c.start()

    chunk = 256
    tchunks = tokens // chunk

    def gradients(h):
        cols = pl.ds(pl.multiple_of(h * HEAD, HEAD), HEAD)
        grad[h] = jnp.zeros((rows3, HEAD), F32)
        gw = gate_ref[h].astype(BF16)
        lw = lift_ref[h].astype(BF16)
        dw = down_ref[h].astype(BF16)
        gchunk = 512

        def body(i, carry):
            rows = pl.ds(pl.multiple_of(i * gchunk, gchunk), gchunk)
            kk = k_ref[rows, cols]
            vv = v_ref[rows, cols].astype(F32)
            rr = rate_ref[rows, :]
            pick = lax.broadcasted_iota(jnp.int32, rr.shape, 1) == h
            rate = jnp.sum(jnp.where(pick, rr, 0.0), axis=1, keepdims=True)
            target = (-rate * vv).astype(BF16)
            gp = dot(kk, gw)
            lp = dot(kk, lw)
            sg = jax.nn.sigmoid(gp)
            act = gp * sg
            hidden = (act * lp).astype(BF16)
            grad[h, 2 * HEAD : 3 * HEAD, :] += dot(hidden, target, 0, 0)
            bh = dot(target, dw, 1, 1)
            bg = (bh * lp * sg * (1.0 + gp * (1.0 - sg))).astype(BF16)
            bl = (bh * act).astype(BF16)
            grad[h, 0:HEAD, :] += dot(kk, bg, 0, 0)
            grad[h, HEAD : 2 * HEAD, :] += dot(kk, bl, 0, 0)
            return carry

        lax.fori_loop(0, tokens // gchunk, body, 0)

    scale = HEAD ** (-0.5)

    def local_attention(h):
        cols = pl.ds(h * HEAD, HEAD)
        for i in range(tchunks):
            rows = pl.ds(i * chunk, chunk)
            span = (i + 1) * chunk
            s = dot(q_ref[rows, cols], k_ref[0:span, cols], 1, 1) * scale
            qi = lax.broadcasted_iota(jnp.int32, s.shape, 0) + i * chunk
            ki = lax.broadcasted_iota(jnp.int32, s.shape, 1)
            s = jnp.where(ki <= qi, s, MASKED)
            m = jnp.max(s, axis=1, keepdims=True)
            p = jnp.exp(s - m)
            m_ref[h, rows, :] = m
            l_ref[h, rows, :] = jnp.sum(p, axis=1, keepdims=True)
            att[rows, cols] = dot(p.astype(BF16), v_ref[0:span, cols])

    def halo_attention(h):
        cols = pl.ds(h * HEAD, HEAD)

        @pl.when(me > 0)
        def _():
            for c in halo_copies(h):
                c.wait_recv()
            for i in range(tchunks):
                rows = pl.ds(i * chunk, chunk)
                keys = pl.ds(i * chunk, WINDOW - i * chunk)
                s = dot(q_ref[rows, cols], ek[keys, cols], 1, 1) * scale
                qi = lax.broadcasted_iota(jnp.int32, s.shape, 0)
                ki = lax.broadcasted_iota(jnp.int32, s.shape, 1)
                s = jnp.where(ki > qi, s, MASKED)
                m_old = m_ref[h, rows, :]
                m = jnp.maximum(m_old, jnp.max(s, axis=1, keepdims=True))
                p = jnp.exp(s - m)
                fix = jnp.exp(m_old - m)
                l_ref[h, rows, :] = l_ref[h, rows, :] * fix + jnp.sum(p, axis=1, keepdims=True)
                att[rows, cols] = att[rows, cols] * fix + dot(p.astype(BF16), ev[keys, cols])

    gradients(1 - core)
    core_send[...] = grad[1 - core].astype(BF16)
    core_copy = pltpu.make_async_remote_copy(
        src_ref=core_send, dst_ref=core_recv, send_sem=core_s, recv_sem=core_r,
        device_id={"seq": partner(1)}, device_id_type=MESH,
    )
    core_copy.start()
    gradients(core)
    core_copy.wait()

    work = [lambda: local_attention(0), lambda: local_attention(1)]
    late = [lambda: halo_attention(0), lambda: halo_attention(1)]
    off = 0 * me
    size = rows3
    base = 0
    spans = []
    previous = None
    for t, d in enumerate(steps):
        half = size // 2
        keep = pl.multiple_of(off + bit(d) * half, 16)
        give = pl.multiple_of(off + (1 - bit(d)) * half, 16)
        for at in (give, keep):
            r = pl.ds(at, half)
            if t == 0:
                grad[core, r, :] += core_recv[r, :].astype(F32)
            else:
                pr = pl.ds(pl.multiple_of(at - off, 16) + previous, half)
                grad[core, r, :] += rs_recv[pr, :].astype(F32)
            if at is give:
                rs_send[base : base + half, :] = grad[core, r, :].astype(BF16)
                copy = pltpu.make_async_remote_copy(
                    src_ref=rs_send.at[base : base + half], dst_ref=rs_recv.at[base : base + half],
                    send_sem=rs_s.at[t], recv_sem=rs_r.at[t],
                    device_id={"seq": partner(d)}, device_id_type=MESH,
                )
                copy.start()
        if work:
            work.pop(0)()
        copy.wait()
        spans.append((off, size))
        off, size = keep, half
        previous = base
        base += half
    own = pl.ds(off, size)
    gsum[own, :] = (
        grad[core, own, :] + rs_recv[previous : previous + size, :].astype(F32)
    ).astype(BF16)
    for t in reversed(range(len(steps))):
        d = steps[t]
        mine = pl.ds(off, size)
        copy = pltpu.make_async_remote_copy(
            src_ref=gsum.at[mine], dst_ref=gsum.at[mine],
            send_sem=ag_s.at[t], recv_sem=ag_r.at[t],
            device_id={"seq": partner(d)}, device_id_type=MESH,
        )
        copy.start()
        if work:
            work.pop(0)()
        elif late and t < 2:
            late.pop(0)()
        copy.wait()
        off, size = spans[t]
    eye = (
        lax.broadcasted_iota(jnp.int32, (HEAD, HEAD), 0)
        == lax.broadcasted_iota(jnp.int32, (HEAD, HEAD), 1)
    )
    for w, w_ref in enumerate((gate_ref, lift_ref, down_ref)):
        g = gsum[w * HEAD : (w + 1) * HEAD, :].astype(F32)
        trace = jnp.sum(jnp.sum(g * g, axis=1, keepdims=True), axis=0, keepdims=True) + EPSILON
        x = (g * lax.rsqrt(trace)).astype(BF16)
        for sweep in range(NS_STEPS):
            a = dot(x, x, 0, 0)
            b = a.astype(BF16)
            poly = COEF_B * a + COEF_C * dot(b, b) + jnp.where(eye, COEF_A, 0.0)
            x = dot(x, poly.astype(BF16)).astype(BF16)
        old = w_ref[core]
        change = old - x.astype(F32)
        old_sq = jnp.sum(old * old, axis=0, keepdims=True)
        new_sq = jnp.sum(change * change, axis=0, keepdims=True)
        new_w[core, w] = (change * jnp.sqrt(old_sq / (new_sq + EPSILON))).astype(BF16)
    nw_copy = pltpu.make_async_remote_copy(
        src_ref=new_w.at[core], dst_ref=new_w.at[core], send_sem=nw_s, recv_sem=nw_r,
        device_id={"seq": partner(1)}, device_id_type=MESH,
    )
    nw_copy.start()
    for f in work + late:
        f()
    nw_copy.wait()

    y_copies = []
    for i in range(tchunks):
        rows = pl.ds(i * chunk, chunk)
        parts = []
        for h in range(heads):
            cols = pl.ds(h * HEAD, HEAD)
            qq = q_ref[rows, cols]
            gp = dot(qq, new_w[h, 0])
            lp = dot(qq, new_w[h, 1])
            hid = (gp * jax.nn.sigmoid(gp) * lp).astype(BF16)
            mem = dot(hid, new_w[h, 2])
            ms = jnp.mean(mem * mem, axis=1, keepdims=True)
            normed = mem * lax.rsqrt(ms + EPSILON) * gain_ref[h : h + 1, :]
            parts.append((att[rows, cols] / l_ref[h, rows, :] + normed).astype(BF16))
        theirs = pl.ds(pl.multiple_of((1 - y) * out_cols, out_cols), out_cols)
        ours = pl.ds(pl.multiple_of(y * out_cols, out_cols), out_cols)

        def project(cs):
            total = dot(parts[0], ow_ref[0:HEAD, cs])
            for h in range(1, heads):
                total += dot(parts[h], ow_ref[h * HEAD : (h + 1) * HEAD, cs])
            return total

        psend[rows, :] = project(theirs).astype(BF16)
        copy = pltpu.make_async_remote_copy(
            src_ref=psend.at[rows], dst_ref=precv.at[rows], send_sem=y_s.at[i],
            recv_sem=y_r.at[i], device_id={"head": 1 - y}, device_id_type=MESH,
        )
        copy.start()
        y_copies.append(copy)
        o_ref[rows, :] = project(ours).astype(BF16)
    for i in range(tchunks):
        rows = pl.ds(i * chunk, chunk)
        y_copies[i].wait()
        o_ref[rows, :] = (o_ref[rows, :].astype(F32) + precv[rows, :].astype(F32)).astype(BF16)

    @pl.when(me < n - 1)
    def _():
        for h in range(heads):
            for c in halo_copies(h):
                c.wait_send()


def solution(mesh):
    n = mesh.shape["seq"]
    groups = mesh.shape["head"]

    def shards(q, k, v, rates, gate, lift, down, gain, ow):
        tokens, width = q.shape
        heads = gate.shape[0]
        out_cols = ow.shape[1] // groups
        assert heads == 2 and groups == 2 and tokens == WINDOW
        rows3 = 3 * HEAD
        nsteps = n.bit_length() - 2
        dma = pltpu.SemaphoreType.DMA
        return pl.pallas_call(
            functools.partial(kernel, n, tokens, heads, out_cols),
            out_shape=jax.ShapeDtypeStruct((tokens, out_cols), BF16),
            in_specs=[pl.BlockSpec(memory_space=pltpu.VMEM)] * 9,
            out_specs=pl.BlockSpec(memory_space=pltpu.VMEM),
            scratch_shapes=[
                pltpu.VMEM((tokens, width), BF16),
                pltpu.VMEM((tokens, width), BF16),
                pltpu.VMEM((heads, rows3, HEAD), F32),
                pltpu.VMEM((rows3, HEAD), BF16),
                pltpu.VMEM((rows3, HEAD), BF16),
                pltpu.VMEM((rows3, HEAD), BF16),
                pltpu.VMEM((rows3, HEAD), BF16),
                pltpu.VMEM((rows3, HEAD), BF16),
                pltpu.VMEM((tokens, width), F32),
                pltpu.VMEM((heads, tokens, 1), F32),
                pltpu.VMEM((heads, tokens, 1), F32),
                pltpu.VMEM((heads, 3, HEAD, HEAD), BF16),
                pltpu.VMEM((tokens, out_cols), BF16),
                pltpu.VMEM((tokens, out_cols), BF16),
                dma((2 * heads,)), dma((2 * heads,)),
                dma, dma,
                dma((nsteps,)), dma((nsteps,)),
                dma((nsteps,)), dma((nsteps,)),
                dma, dma,
                dma((tokens // 256,)), dma((tokens // 256,)),
            ],
            compiler_params=pltpu.CompilerParams(
                collective_id=0, has_side_effects=True, vmem_limit_bytes=62 * 1024 * 1024
            ),
            cost_estimate=pl.CostEstimate(
                flops=30 * 10**9, bytes_accessed=20 * 2**20, transcendentals=10**7
            ),
        )(q, k, v, rates.T, gate, lift, down, gain, ow)

    return jax.shard_map(
        shards,
        mesh=mesh,
        in_specs=(
            P("seq", "head"),
            P("seq", "head"),
            P("seq", "head"),
            P("head", "seq"),
            P("head", None, None),
            P("head", None, None),
            P("head", None, None),
            P("head", None),
            P("head", None),
        ),
        out_specs=P("seq", "head"),
        check_vma=False,
    )
```

```python
import functools

import jax
import jax.numpy as jnp
from jax import lax
from jax.experimental import pallas as pl
from jax.experimental.pallas import tpu as pltpu
from jax.sharding import PartitionSpec as P

HEAD = 512
WINDOW = 1024
NS_STEPS = 2
COEF_A = 3.4445
COEF_B = -4.775
COEF_C = 2.0315
EPSILON = 1e-06
MESH = pl.DeviceIdType.MESH
F32 = jnp.float32
BF16 = jnp.bfloat16
MASKED = -1e30


def dot(a, b, ca=1, cb=0):
    return lax.dot_general(a, b, (((ca,), (cb,)), ((), ())), preferred_element_type=F32)


def kernel(
    n, tokens, heads, out_cols,
    q_ref, k_ref, v_ref, rate_ref, gate_ref, lift_ref, down_ref, gain_ref, ow_ref, o_ref,
    ek, ev, grad, core_send, core_recv, rs_send, rs_recv, gsum, att, m_ref, l_ref, new_w,
    psend, precv,
    halo_s, halo_r, core_s, core_r, rs_s, rs_r, ag_s, ag_r, nw_s, nw_r, y_s, y_r,
):
    me = lax.axis_index("seq")
    y = lax.axis_index("head")
    rows3 = 3 * HEAD
    core = me % 2
    steps = []
    d = 2
    while d < n:
        steps.append(d)
        d *= 2
    nsteps = len(steps)
    orders = [steps, steps[1:] + steps[:1], steps[:1] + steps[:0:-1]]

    def bit(d):
        return (me // d) % 2

    def partner(d):
        return me + d * (1 - 2 * bit(d))

    barrier = pltpu.get_barrier_semaphore()
    peers = [{"seq": (me + 1) % n}, {"seq": (me + n - 1) % n}, {"head": 1 - y}]
    peers += [{"seq": partner(d)} for d in [1] + steps]
    for peer in peers:
        pl.semaphore_signal(barrier, inc=1, device_id=peer, device_id_type=MESH)
    pl.semaphore_wait(barrier, len(peers))

    chunk = 256
    tchunks = tokens // chunk

    def halo_copies(c):
        rows = pl.ds(c * chunk, chunk)
        return [
            pltpu.make_async_remote_copy(
                src_ref=src.at[rows], dst_ref=dst.at[rows],
                send_sem=halo_s.at[2 * c + j], recv_sem=halo_r.at[2 * c + j],
                device_id={"seq": (me + 1) % n}, device_id_type=MESH,
            )
            for j, (src, dst) in enumerate(((k_ref, ek), (v_ref, ev)))
        ]

    def start_halo(chunks):
        @pl.when(me < n - 1)
        def _():
            for c in chunks:
                for copy in halo_copies(c):
                    copy.start()

    early = tchunks // 2
    start_halo(range(tchunks - 1, early - 1, -1))

    def gradients(h):
        cols = pl.ds(pl.multiple_of(h * HEAD, HEAD), HEAD)
        grad[h] = jnp.zeros((rows3, HEAD), F32)
        gw = gate_ref[h].astype(BF16)
        lw = lift_ref[h].astype(BF16)
        dw = down_ref[h].astype(BF16)
        gchunk = 512

        def body(i, carry):
            rows = pl.ds(pl.multiple_of(i * gchunk, gchunk), gchunk)
            kk = k_ref[rows, cols]
            vv = v_ref[rows, cols].astype(F32)
            rr = rate_ref[rows, :]
            pick = lax.broadcasted_iota(jnp.int32, rr.shape, 1) == h
            rate = jnp.sum(jnp.where(pick, rr, 0.0), axis=1, keepdims=True)
            target = (-rate * vv).astype(BF16)
            gp = dot(kk, gw)
            lp = dot(kk, lw)
            sg = jax.nn.sigmoid(gp)
            act = gp * sg
            hidden = (act * lp).astype(BF16)
            grad[h, 2 * HEAD : 3 * HEAD, :] += dot(hidden, target, 0, 0)
            bh = dot(target, dw, 1, 1)
            bg = (bh * lp * sg * (1.0 + gp * (1.0 - sg))).astype(BF16)
            bl = (bh * act).astype(BF16)
            grad[h, 0:HEAD, :] += dot(kk, bg, 0, 0)
            grad[h, HEAD : 2 * HEAD, :] += dot(kk, bl, 0, 0)
            return carry

        lax.fori_loop(0, tokens // gchunk, body, 0)

    scale = HEAD ** (-0.5)

    def local_attention(h):
        cols = pl.ds(h * HEAD, HEAD)
        for i in range(tchunks):
            rows = pl.ds(i * chunk, chunk)
            span = (i + 1) * chunk
            s = dot(q_ref[rows, cols], k_ref[0:span, cols], 1, 1) * scale
            qi = lax.broadcasted_iota(jnp.int32, s.shape, 0) + i * chunk
            ki = lax.broadcasted_iota(jnp.int32, s.shape, 1)
            s = jnp.where(ki <= qi, s, MASKED)
            m = jnp.max(s, axis=1, keepdims=True)
            p = jnp.exp(s - m)
            m_ref[h, rows, :] = m
            l_ref[h, rows, :] = jnp.sum(p, axis=1, keepdims=True)
            att[rows, cols] = dot(p.astype(BF16), v_ref[0:span, cols])

    def halo_attention(i):
        @pl.when(me > 0)
        def _():
            for c in halo_copies(i):
                c.wait_recv()
            rows = pl.ds(i * chunk, chunk)
            keys = pl.ds(i * chunk, WINDOW - i * chunk)
            for h in range(heads):
                cols = pl.ds(h * HEAD, HEAD)
                s = dot(q_ref[rows, cols], ek[keys, cols], 1, 1) * scale
                qi = lax.broadcasted_iota(jnp.int32, s.shape, 0)
                ki = lax.broadcasted_iota(jnp.int32, s.shape, 1)
                s = jnp.where(ki > qi, s, MASKED)
                m_old = m_ref[h, rows, :]
                m = jnp.maximum(m_old, jnp.max(s, axis=1, keepdims=True))
                p = jnp.exp(s - m)
                fix = jnp.exp(m_old - m)
                l_ref[h, rows, :] = l_ref[h, rows, :] * fix + jnp.sum(p, axis=1, keepdims=True)
                att[rows, cols] = att[rows, cols] * fix + dot(p.astype(BF16), ev[keys, cols])

    gradients(1 - core)
    core_send[...] = grad[1 - core].astype(BF16)
    core_copy = pltpu.make_async_remote_copy(
        src_ref=core_send, dst_ref=core_recv, send_sem=core_s, recv_sem=core_r,
        device_id={"seq": partner(1)}, device_id_type=MESH,
    )
    core_copy.start()
    gradients(core)
    core_copy.wait()

    work = [lambda: local_attention(0), lambda: local_attention(1)]
    late = list(range(tchunks - 1, -1, -1))
    offs = [w * HEAD + 0 * me for w in range(3)]
    sizes = [HEAD] * 3
    bases = [w * HEAD for w in range(3)]
    previous = [None] * 3
    spans = [[], [], []]
    copies = [None] * 3
    for t in range(nsteps):
        for w in range(3):
            d = orders[w][t]
            off, half, base = offs[w], sizes[w] // 2, bases[w]
            keep = pl.multiple_of(off + bit(d) * half, 16)
            give = pl.multiple_of(off + (1 - bit(d)) * half, 16)
            if t > 0:
                copies[w].wait()
            for first, at in ((True, give), (False, keep)):
                r = pl.ds(at, half)
                if t == 0:
                    grad[core, r, :] += core_recv[r, :].astype(F32)
                else:
                    pr = pl.ds(pl.multiple_of(at - off, 16) + previous[w], half)
                    grad[core, r, :] += rs_recv[pr, :].astype(F32)
                if first:
                    rs_send[base : base + half, :] = grad[core, r, :].astype(BF16)
                    copies[w] = pltpu.make_async_remote_copy(
                        src_ref=rs_send.at[base : base + half],
                        dst_ref=rs_recv.at[base : base + half],
                        send_sem=rs_s.at[w * nsteps + t], recv_sem=rs_r.at[w * nsteps + t],
                        device_id={"seq": partner(d)}, device_id_type=MESH,
                    )
                    copies[w].start()
            spans[w].append((off, sizes[w]))
            offs[w], sizes[w] = keep, half
            previous[w] = base
            bases[w] += half
        if work:
            work.pop(0)()
    for t in reversed(range(nsteps)):
        for w in range(3):
            copies[w].wait()
            if t == nsteps - 1:
                own = pl.ds(offs[w], sizes[w])
                gsum[own, :] = (
                    grad[core, own, :]
                    + rs_recv[previous[w] : previous[w] + sizes[w], :].astype(F32)
                ).astype(BF16)
            else:
                offs[w], sizes[w] = spans[w][t + 1]
            mine = pl.ds(offs[w], sizes[w])
            copies[w] = pltpu.make_async_remote_copy(
                src_ref=gsum.at[mine], dst_ref=gsum.at[mine],
                send_sem=ag_s.at[w * nsteps + t], recv_sem=ag_r.at[w * nsteps + t],
                device_id={"seq": partner(orders[w][t])}, device_id_type=MESH,
            )
            copies[w].start()
        if work:
            work.pop(0)()
        elif late and late[0] >= early:
            halo_attention(late.pop(0))
    for f in work:
        f()
    eye = (
        lax.broadcasted_iota(jnp.int32, (HEAD, HEAD), 0)
        == lax.broadcasted_iota(jnp.int32, (HEAD, HEAD), 1)
    )
    nw_copies = []
    for w, w_ref in enumerate((gate_ref, lift_ref, down_ref)):
        copies[w].wait()
        if w == 2:
            start_halo(range(early - 1, -1, -1))
        g = gsum[w * HEAD : (w + 1) * HEAD, :].astype(F32)
        trace = jnp.sum(jnp.sum(g * g, axis=1, keepdims=True), axis=0, keepdims=True) + EPSILON
        x = (g * lax.rsqrt(trace)).astype(BF16)
        for sweep in range(NS_STEPS):
            a = dot(x, x, 0, 0)
            b = a.astype(BF16)
            poly = COEF_B * a + COEF_C * dot(b, b) + jnp.where(eye, COEF_A, 0.0)
            x = dot(x, poly.astype(BF16)).astype(BF16)
        old = w_ref[core]
        change = old - x.astype(F32)
        old_sq = jnp.sum(old * old, axis=0, keepdims=True)
        new_sq = jnp.sum(change * change, axis=0, keepdims=True)
        new_w[core, w] = (change * jnp.sqrt(old_sq / (new_sq + EPSILON))).astype(BF16)
        nw_copy = pltpu.make_async_remote_copy(
            src_ref=new_w.at[core, w], dst_ref=new_w.at[core, w],
            send_sem=nw_s.at[w], recv_sem=nw_r.at[w],
            device_id={"seq": partner(1)}, device_id_type=MESH,
        )
        nw_copy.start()
        nw_copies.append(nw_copy)
    for copy in nw_copies:
        copy.wait()

    y_copies = [None] * tchunks
    for i in reversed(range(tchunks)):
        if i in late:
            halo_attention(i)
        rows = pl.ds(i * chunk, chunk)
        parts = []
        for h in range(heads):
            cols = pl.ds(h * HEAD, HEAD)
            qq = q_ref[rows, cols]
            gp = dot(qq, new_w[h, 0])
            lp = dot(qq, new_w[h, 1])
            hid = (gp * jax.nn.sigmoid(gp) * lp).astype(BF16)
            mem = dot(hid, new_w[h, 2])
            ms = jnp.mean(mem * mem, axis=1, keepdims=True)
            normed = mem * lax.rsqrt(ms + EPSILON) * gain_ref[h : h + 1, :]
            parts.append((att[rows, cols] / l_ref[h, rows, :] + normed).astype(BF16))
        theirs = pl.ds(pl.multiple_of((1 - y) * out_cols, out_cols), out_cols)
        ours = pl.ds(pl.multiple_of(y * out_cols, out_cols), out_cols)

        def project(cs):
            total = dot(parts[0], ow_ref[0:HEAD, cs])
            for h in range(1, heads):
                total += dot(parts[h], ow_ref[h * HEAD : (h + 1) * HEAD, cs])
            return total

        psend[rows, :] = project(theirs).astype(BF16)
        copy = pltpu.make_async_remote_copy(
            src_ref=psend.at[rows], dst_ref=precv.at[rows], send_sem=y_s.at[i],
            recv_sem=y_r.at[i], device_id={"head": 1 - y}, device_id_type=MESH,
        )
        copy.start()
        y_copies[i] = copy
        o_ref[rows, :] = project(ours).astype(BF16)
    for i in reversed(range(tchunks)):
        rows = pl.ds(i * chunk, chunk)
        y_copies[i].wait()
        o_ref[rows, :] = (o_ref[rows, :].astype(F32) + precv[rows, :].astype(F32)).astype(BF16)

    @pl.when(me < n - 1)
    def _():
        for i in range(tchunks):
            for c in halo_copies(i):
                c.wait_send()


def solution(mesh):
    n = mesh.shape["seq"]
    groups = mesh.shape["head"]

    def shards(q, k, v, rates, gate, lift, down, gain, ow):
        tokens, width = q.shape
        heads = gate.shape[0]
        out_cols = ow.shape[1] // groups
        assert heads == 2 and groups == 2 and tokens == WINDOW
        rows3 = 3 * HEAD
        nsteps = n.bit_length() - 2
        dma = pltpu.SemaphoreType.DMA
        return pl.pallas_call(
            functools.partial(kernel, n, tokens, heads, out_cols),
            out_shape=jax.ShapeDtypeStruct((tokens, out_cols), BF16),
            in_specs=[pl.BlockSpec(memory_space=pltpu.VMEM)] * 9,
            out_specs=pl.BlockSpec(memory_space=pltpu.VMEM),
            scratch_shapes=[
                pltpu.VMEM((tokens, width), BF16),
                pltpu.VMEM((tokens, width), BF16),
                pltpu.VMEM((heads, rows3, HEAD), F32),
                pltpu.VMEM((rows3, HEAD), BF16),
                pltpu.VMEM((rows3, HEAD), BF16),
                pltpu.VMEM((rows3, HEAD), BF16),
                pltpu.VMEM((rows3, HEAD), BF16),
                pltpu.VMEM((rows3, HEAD), BF16),
                pltpu.VMEM((tokens, width), F32),
                pltpu.VMEM((heads, tokens, 1), F32),
                pltpu.VMEM((heads, tokens, 1), F32),
                pltpu.VMEM((heads, 3, HEAD, HEAD), BF16),
                pltpu.VMEM((tokens, out_cols), BF16),
                pltpu.VMEM((tokens, out_cols), BF16),
                dma((2 * tokens // 256,)), dma((2 * tokens // 256,)),
                dma, dma,
                dma((3 * nsteps,)), dma((3 * nsteps,)),
                dma((3 * nsteps,)), dma((3 * nsteps,)),
                dma((3,)), dma((3,)),
                dma((tokens // 256,)), dma((tokens // 256,)),
            ],
            compiler_params=pltpu.CompilerParams(
                collective_id=0, has_side_effects=True, vmem_limit_bytes=62 * 1024 * 1024
            ),
            cost_estimate=pl.CostEstimate(
                flops=30 * 10**9, bytes_accessed=20 * 2**20, transcendentals=10**7
            ),
        )(q, k, v, rates.T, gate, lift, down, gain, ow)

    return jax.shard_map(
        shards,
        mesh=mesh,
        in_specs=(
            P("seq", "head"),
            P("seq", "head"),
            P("seq", "head"),
            P("head", "seq"),
            P("head", None, None),
            P("head", None, None),
            P("head", None, None),
            P("head", None),
            P("head", None),
        ),
        out_specs=P("seq", "head"),
        check_vma=False,
    )
```

```python
import functools

import jax
import jax.numpy as jnp
from jax import lax
from jax.experimental import pallas as pl
from jax.experimental.pallas import tpu as pltpu
from jax.sharding import PartitionSpec as P

HEAD = 512
WINDOW = 1024
NS_STEPS = 2
COEF_A = 3.4445
COEF_B = -4.775
COEF_C = 2.0315
EPSILON = 1e-06
MESH = pl.DeviceIdType.MESH
F32 = jnp.float32
BF16 = jnp.bfloat16
MASKED = -1e30


def dot(a, b, ca=1, cb=0):
    return lax.dot_general(a, b, (((ca,), (cb,)), ((), ())), preferred_element_type=F32)


def kernel(
    n, tokens, heads, out_cols,
    q_ref, k_ref, v_ref, rate_ref, gate_ref, lift_ref, down_ref, gain_ref, ow_ref, o_ref,
    ek, ev, grad, core_send, core_recv, rs_send, rs_recv, gsum, att, m_ref, l_ref, new_w,
    psend, precv,
    halo_s, halo_r, core_s, core_r, rs_s, rs_r, ag_s, ag_r, nw_s, nw_r, y_s, y_r,
):
    me = lax.axis_index("seq")
    y = lax.axis_index("head")
    rows3 = 3 * HEAD
    core = me % 2
    steps = []
    d = 2
    while d < n:
        steps.append(d)
        d *= 2
    nsteps = len(steps)
    orders = [steps[i:] + steps[:i] for i in (0, 1, 2)]

    def bit(d):
        return (me // d) % 2

    def partner(d):
        return me + d * (1 - 2 * bit(d))

    barrier = pltpu.get_barrier_semaphore()
    peers = [{"seq": (me + 1) % n}, {"seq": (me + n - 1) % n}, {"head": 1 - y}]
    peers += [{"seq": partner(d)} for d in [1] + steps]
    for peer in peers:
        pl.semaphore_signal(barrier, inc=1, device_id=peer, device_id_type=MESH)
    pl.semaphore_wait(barrier, len(peers))

    chunk = 256
    tchunks = tokens // chunk

    def halo_copies(c):
        rows = pl.ds(c * chunk, chunk)
        return [
            pltpu.make_async_remote_copy(
                src_ref=src.at[rows], dst_ref=dst.at[rows],
                send_sem=halo_s.at[2 * c + j], recv_sem=halo_r.at[2 * c + j],
                device_id={"seq": (me + 1) % n}, device_id_type=MESH,
            )
            for j, (src, dst) in enumerate(((k_ref, ek), (v_ref, ev)))
        ]

    def start_halo(chunks):
        @pl.when(me < n - 1)
        def _():
            for c in chunks:
                for copy in halo_copies(c):
                    copy.start()

    early = 3*tchunks//4
    start_halo(range(tchunks - 1, early - 1, -1))

    def gradients(h):
        cols = pl.ds(pl.multiple_of(h * HEAD, HEAD), HEAD)
        grad[h] = jnp.zeros((rows3, HEAD), F32)
        gw = gate_ref[h].astype(BF16)
        lw = lift_ref[h].astype(BF16)
        dw = down_ref[h].astype(BF16)
        gchunk = 512

        def body(i, carry):
            rows = pl.ds(pl.multiple_of(i * gchunk, gchunk), gchunk)
            kk = k_ref[rows, cols]
            vv = v_ref[rows, cols].astype(F32)
            rr = rate_ref[rows, :]
            pick = lax.broadcasted_iota(jnp.int32, rr.shape, 1) == h
            rate = jnp.sum(jnp.where(pick, rr, 0.0), axis=1, keepdims=True)
            target = (-rate * vv).astype(BF16)
            gp = dot(kk, gw)
            lp = dot(kk, lw)
            sg = jax.nn.sigmoid(gp)
            act = gp * sg
            hidden = (act * lp).astype(BF16)
            grad[h, 2 * HEAD : 3 * HEAD, :] += dot(hidden, target, 0, 0)
            bh = dot(target, dw, 1, 1)
            bg = (bh * lp * sg * (1.0 + gp * (1.0 - sg))).astype(BF16)
            bl = (bh * act).astype(BF16)
            grad[h, 0:HEAD, :] += dot(kk, bg, 0, 0)
            grad[h, HEAD : 2 * HEAD, :] += dot(kk, bl, 0, 0)
            return carry

        lax.fori_loop(0, tokens // gchunk, body, 0)

    scale = HEAD ** (-0.5)

    def local_attention(h):
        cols = pl.ds(h * HEAD, HEAD)
        for i in range(tchunks):
            rows = pl.ds(i * chunk, chunk)
            span = (i + 1) * chunk
            s = dot(q_ref[rows, cols], k_ref[0:span, cols], 1, 1) * scale
            qi = lax.broadcasted_iota(jnp.int32, s.shape, 0) + i * chunk
            ki = lax.broadcasted_iota(jnp.int32, s.shape, 1)
            s = jnp.where(ki <= qi, s, MASKED)
            m = jnp.max(s, axis=1, keepdims=True)
            p = jnp.exp(s - m)
            m_ref[h, rows, :] = m
            l_ref[h, rows, :] = jnp.sum(p, axis=1, keepdims=True)
            att[rows, cols] = dot(p.astype(BF16), v_ref[0:span, cols])

    def halo_attention(i):
        @pl.when(me > 0)
        def _():
            for c in halo_copies(i):
                c.wait_recv()
            rows = pl.ds(i * chunk, chunk)
            keys = pl.ds(i * chunk, WINDOW - i * chunk)
            for h in range(heads):
                cols = pl.ds(h * HEAD, HEAD)
                s = dot(q_ref[rows, cols], ek[keys, cols], 1, 1) * scale
                qi = lax.broadcasted_iota(jnp.int32, s.shape, 0)
                ki = lax.broadcasted_iota(jnp.int32, s.shape, 1)
                s = jnp.where(ki > qi, s, MASKED)
                m_old = m_ref[h, rows, :]
                m = jnp.maximum(m_old, jnp.max(s, axis=1, keepdims=True))
                p = jnp.exp(s - m)
                fix = jnp.exp(m_old - m)
                l_ref[h, rows, :] = l_ref[h, rows, :] * fix + jnp.sum(p, axis=1, keepdims=True)
                att[rows, cols] = att[rows, cols] * fix + dot(p.astype(BF16), ev[keys, cols])

    gradients(1 - core)
    core_send[...] = grad[1 - core].astype(BF16)
    core_copy = pltpu.make_async_remote_copy(
        src_ref=core_send, dst_ref=core_recv, send_sem=core_s, recv_sem=core_r,
        device_id={"seq": partner(1)}, device_id_type=MESH,
    )
    core_copy.start()
    gradients(core)
    core_copy.wait()

    work = [lambda: local_attention(0), lambda: local_attention(1)]
    late = list(range(tchunks - 1, -1, -1))
    offs = [w * HEAD + 0 * me for w in range(3)]
    sizes = [HEAD] * 3
    bases = [w * HEAD for w in range(3)]
    previous = [None] * 3
    spans = [[], [], []]
    copies = [None] * 3
    for t in range(nsteps):
        for w in range(3):
            d = orders[w][t]
            off, half, base = offs[w], sizes[w] // 2, bases[w]
            keep = pl.multiple_of(off + bit(d) * half, 16)
            give = pl.multiple_of(off + (1 - bit(d)) * half, 16)
            if t > 0:
                copies[w].wait()
            for first, at in ((True, give), (False, keep)):
                r = pl.ds(at, half)
                if t == 0:
                    grad[core, r, :] += core_recv[r, :].astype(F32)
                else:
                    pr = pl.ds(pl.multiple_of(at - off, 16) + previous[w], half)
                    grad[core, r, :] += rs_recv[pr, :].astype(F32)
                if first:
                    rs_send[base : base + half, :] = grad[core, r, :].astype(BF16)
                    copies[w] = pltpu.make_async_remote_copy(
                        src_ref=rs_send.at[base : base + half],
                        dst_ref=rs_recv.at[base : base + half],
                        send_sem=rs_s.at[w * nsteps + t], recv_sem=rs_r.at[w * nsteps + t],
                        device_id={"seq": partner(d)}, device_id_type=MESH,
                    )
                    copies[w].start()
            spans[w].append((off, sizes[w]))
            offs[w], sizes[w] = keep, half
            previous[w] = base
            bases[w] += half
        if work:
            work.pop(0)()
    for t in reversed(range(nsteps)):
        for w in range(3):
            copies[w].wait()
            if t == nsteps - 1:
                own = pl.ds(offs[w], sizes[w])
                gsum[own, :] = (
                    grad[core, own, :]
                    + rs_recv[previous[w] : previous[w] + sizes[w], :].astype(F32)
                ).astype(BF16)
            else:
                offs[w], sizes[w] = spans[w][t + 1]
            mine = pl.ds(offs[w], sizes[w])
            copies[w] = pltpu.make_async_remote_copy(
                src_ref=gsum.at[mine], dst_ref=gsum.at[mine],
                send_sem=ag_s.at[w * nsteps + t], recv_sem=ag_r.at[w * nsteps + t],
                device_id={"seq": partner(orders[w][t])}, device_id_type=MESH,
            )
            copies[w].start()
        if work:
            work.pop(0)()
        elif late and late[0] >= early:
            halo_attention(late.pop(0))
    for f in work:
        f()
    eye = (
        lax.broadcasted_iota(jnp.int32, (HEAD, HEAD), 0)
        == lax.broadcasted_iota(jnp.int32, (HEAD, HEAD), 1)
    )
    nw_copies = []
    for w, w_ref in enumerate((gate_ref, lift_ref, down_ref)):
        copies[w].wait()
        if w == 2:
            start_halo(range(early - 1, -1, -1))
        g = gsum[w * HEAD : (w + 1) * HEAD, :].astype(F32)
        trace = jnp.sum(jnp.sum(g * g, axis=1, keepdims=True), axis=0, keepdims=True) + EPSILON
        x = (g * lax.rsqrt(trace)).astype(BF16)
        for sweep in range(NS_STEPS):
            a = dot(x, x, 0, 0)
            b = a.astype(BF16)
            poly = COEF_B * a + COEF_C * dot(b, b) + jnp.where(eye, COEF_A, 0.0)
            x = dot(x, poly.astype(BF16)).astype(BF16)
        old = w_ref[core]
        change = old - x.astype(F32)
        old_sq = jnp.sum(old * old, axis=0, keepdims=True)
        new_sq = jnp.sum(change * change, axis=0, keepdims=True)
        new_w[core, w] = (change * jnp.sqrt(old_sq / (new_sq + EPSILON))).astype(BF16)
        nw_copy = pltpu.make_async_remote_copy(
            src_ref=new_w.at[core, w], dst_ref=new_w.at[core, w],
            send_sem=nw_s.at[w], recv_sem=nw_r.at[w],
            device_id={"seq": partner(1)}, device_id_type=MESH,
        )
        nw_copy.start()
        nw_copies.append(nw_copy)
    for copy in nw_copies:
        copy.wait()

    y_copies = [None] * tchunks
    for i in reversed(range(tchunks)):
        if i in late:
            halo_attention(i)
        rows = pl.ds(i * chunk, chunk)
        parts = []
        for h in range(heads):
            cols = pl.ds(h * HEAD, HEAD)
            qq = q_ref[rows, cols]
            gp = dot(qq, new_w[h, 0])
            lp = dot(qq, new_w[h, 1])
            hid = (gp * jax.nn.sigmoid(gp) * lp).astype(BF16)
            mem = dot(hid, new_w[h, 2])
            ms = jnp.mean(mem * mem, axis=1, keepdims=True)
            normed = mem * lax.rsqrt(ms + EPSILON) * gain_ref[h : h + 1, :]
            parts.append((att[rows, cols] / l_ref[h, rows, :] + normed).astype(BF16))
        theirs = pl.ds(pl.multiple_of((1 - y) * out_cols, out_cols), out_cols)
        ours = pl.ds(pl.multiple_of(y * out_cols, out_cols), out_cols)

        def project(cs):
            total = dot(parts[0], ow_ref[0:HEAD, cs])
            for h in range(1, heads):
                total += dot(parts[h], ow_ref[h * HEAD : (h + 1) * HEAD, cs])
            return total

        psend[rows, :] = project(theirs).astype(BF16)
        copy = pltpu.make_async_remote_copy(
            src_ref=psend.at[rows], dst_ref=precv.at[rows], send_sem=y_s.at[i],
            recv_sem=y_r.at[i], device_id={"head": 1 - y}, device_id_type=MESH,
        )
        copy.start()
        y_copies[i] = copy
        o_ref[rows, :] = project(ours).astype(BF16)
    for i in reversed(range(tchunks)):
        rows = pl.ds(i * chunk, chunk)
        y_copies[i].wait()
        o_ref[rows, :] = (o_ref[rows, :].astype(F32) + precv[rows, :].astype(F32)).astype(BF16)

    @pl.when(me < n - 1)
    def _():
        for i in range(tchunks):
            for c in halo_copies(i):
                c.wait_send()


def solution(mesh):
    n = mesh.shape["seq"]
    groups = mesh.shape["head"]

    def shards(q, k, v, rates, gate, lift, down, gain, ow):
        tokens, width = q.shape
        heads = gate.shape[0]
        out_cols = ow.shape[1] // groups
        assert heads == 2 and groups == 2 and tokens == WINDOW
        rows3 = 3 * HEAD
        nsteps = n.bit_length() - 2
        dma = pltpu.SemaphoreType.DMA
        return pl.pallas_call(
            functools.partial(kernel, n, tokens, heads, out_cols),
            out_shape=jax.ShapeDtypeStruct((tokens, out_cols), BF16),
            in_specs=[pl.BlockSpec(memory_space=pltpu.VMEM)] * 9,
            out_specs=pl.BlockSpec(memory_space=pltpu.VMEM),
            scratch_shapes=[
                pltpu.VMEM((tokens, width), BF16),
                pltpu.VMEM((tokens, width), BF16),
                pltpu.VMEM((heads, rows3, HEAD), F32),
                pltpu.VMEM((rows3, HEAD), BF16),
                pltpu.VMEM((rows3, HEAD), BF16),
                pltpu.VMEM((rows3, HEAD), BF16),
                pltpu.VMEM((rows3, HEAD), BF16),
                pltpu.VMEM((rows3, HEAD), BF16),
                pltpu.VMEM((tokens, width), F32),
                pltpu.VMEM((heads, tokens, 1), F32),
                pltpu.VMEM((heads, tokens, 1), F32),
                pltpu.VMEM((heads, 3, HEAD, HEAD), BF16),
                pltpu.VMEM((tokens, out_cols), BF16),
                pltpu.VMEM((tokens, out_cols), BF16),
                dma((2 * tokens // 256,)), dma((2 * tokens // 256,)),
                dma, dma,
                dma((3 * nsteps,)), dma((3 * nsteps,)),
                dma((3 * nsteps,)), dma((3 * nsteps,)),
                dma((3,)), dma((3,)),
                dma((tokens // 256,)), dma((tokens // 256,)),
            ],
            compiler_params=pltpu.CompilerParams(
                collective_id=0, has_side_effects=True, vmem_limit_bytes=62 * 1024 * 1024
            ),
            cost_estimate=pl.CostEstimate(
                flops=30 * 10**9, bytes_accessed=20 * 2**20, transcendentals=10**7
            ),
        )(q, k, v, rates.T, gate, lift, down, gain, ow)

    return jax.shard_map(
        shards,
        mesh=mesh,
        in_specs=(
            P("seq", "head"),
            P("seq", "head"),
            P("seq", "head"),
            P("head", "seq"),
            P("head", None, None),
            P("head", None, None),
            P("head", None, None),
            P("head", None),
            P("head", None),
        ),
        out_specs=P("seq", "head"),
        check_vma=False,
    )
```
